32 devices in a mesh: ws: 4 (over z), seq: 8 (over y, x, core).
Axes of the slice: x: 2, y: 2, z: 4, core: 2. Of those that a mesh axis runs over, the one named last changes fastest.
Arguments:
- tokens: bfloat16 [4, 3072, 1536], P('ws', 'seq'), may hold values from -16 to 16
- w_same: bfloat16 [1536, 1536], replicated, may hold values from -0.15625 to 0.15625
- w_partner: bfloat16 [1536, 1536], replicated, may hold values from -0.15625 to 0.15625
- w_query: bfloat16 [1536, 1024], replicated, may hold values from -0.15625 to 0.15625
- w_key: bfloat16 [1536, 128], replicated, may hold values from -0.15625 to 0.15625
- w_value: bfloat16 [1536, 192], replicated, may hold values from -0.15625 to 0.15625
- w_out: bfloat16 [1536, 1536], replicated, may hold values from -0.15625 to 0.15625
Outputs:
- attended: bfloat16 [4, 3072, 1536], P('ws', 'seq')
The draws below stay inside these ranges and needn't reach their ends.
All inputs are finite; a program needn't handle non-finite values.
Results may differ from the reference program's by a relative error of at most 0.012.
Values may be sent and summed in bfloat16 or wider, within the bound.
No kernel may reach another device: no remote copies, remote signals or barrier semaphores. Data moves between devices by JAX's collectives and lax.ppermute only.
A program may use at most 192 MiB of HBM per device.

```python
import jax
import jax.numpy as jnp
from jax import lax

D = 1536
HEADS = 8
DK = 128
DV = 192
TOK_DEV = 384
SEQ = 3072
LANES = 4
N_WS = 4
N_SEQ = 8


def draw_tokens(key, part):
    base_key = jax.random.fold_in(jax.random.fold_in(key, 17), 0)
    return jnp.clip(jax.random.normal(base_key, (LANES, SEQ, D)), -6.0, 6.0).astype(jnp.bfloat16)


def normal_values(rng, shape, scale, reach, held_as=jnp.bfloat16):
    result = jax.random.normal(rng, shape, jnp.float32) * scale
    return jnp.minimum(jnp.maximum(result, -reach), reach).astype(held_as)


def setup_inputs(seed: int = 0) -> dict:
    key_of = jax.random.split(jax.random.key(seed), 8)
    return {
        "tokens": draw_tokens(jax.random.fold_in(key_of[7], 71), 0),
        "w_same": normal_values(key_of[1], (D, D), D ** -0.5, 0.15625),
        "w_partner": normal_values(key_of[2], (D, D), D ** -0.5, 0.15625),
        "w_query": normal_values(key_of[3], (D, HEADS * DK), D ** -0.5, 0.15625),
        "w_key": normal_values(key_of[4], (D, DK), D ** -0.5, 0.15625),
        "w_value": normal_values(key_of[5], (D, DV), D ** -0.5, 0.15625),
        "w_out": normal_values(key_of[6], (HEADS * DV, D), (HEADS * DV) ** -0.5, 0.15625),
    }


def attend(query, key, value):
    blocks = query.reshape(N_SEQ, TOK_DEV, HEADS, DK).astype(jnp.float32)
    key_f = key.astype(jnp.float32)
    value_f = value.astype(jnp.float32)
    factor = DK ** -0.5

    def one_block(rows):
        scores = jnp.einsum('qhd,kd->qhk', rows, key_f) * factor
        peak = jnp.max(scores, axis=2, keepdims=True)
        weights = jnp.exp(scores - peak)
        total = jnp.sum(weights, axis=2, keepdims=True)
        rounded = lax.optimization_barrier(weights.astype(jnp.bfloat16)).astype(jnp.float32)
        summed = jnp.einsum('qhk,kd->qhd', rounded, value_f)
        return (summed / total).astype(jnp.bfloat16).reshape(TOK_DEV, HEADS * DV)

    return lax.map(one_block, blocks).reshape(SEQ, HEADS * DV)


def reference(tokens, w_same, w_partner, w_query, w_key, w_value, w_out):
    paired = tokens.reshape(N_WS // 2, 2, SEQ, D)[:, ::-1]
    mirrored = jnp.flip(paired, axis=2).reshape(N_WS * SEQ, D)
    flat = tokens.reshape(N_WS * SEQ, D)
    hidden = (jnp.dot(flat, w_same, preferred_element_type=jnp.float32)
              + jnp.dot(mirrored, w_partner, preferred_element_type=jnp.float32)).astype(jnp.bfloat16)
    query = jnp.dot(hidden, w_query, preferred_element_type=jnp.float32).astype(jnp.bfloat16)
    key = jnp.dot(hidden, w_key, preferred_element_type=jnp.float32).astype(jnp.bfloat16)
    value = jnp.dot(hidden, w_value, preferred_element_type=jnp.float32).astype(jnp.bfloat16)
    query = query.reshape(N_WS, SEQ, HEADS * DK)
    key = key.reshape(N_WS, SEQ, DK)
    value = value.reshape(N_WS, SEQ, DV)
    outputs = []
    for lane in range(N_WS):
        mixed = attend(query[lane], key[lane], value[lane])
        outputs.append(jnp.dot(mixed, w_out, preferred_element_type=jnp.float32).astype(jnp.bfloat16))
    return jnp.stack(outputs, axis=0)
```

```python
import functools
import math

import jax
import jax.numpy as jnp
from jax import lax
from jax.experimental import pallas as pl
from jax.experimental.pallas import tpu as pltpu
from jax.sharding import PartitionSpec as P

F32 = jnp.float32
BF16 = jnp.bfloat16
CONTRACT_LAST = (((1,), (1,)), ((), ()))
CHUNKS = (1,)
VMEM_LIMIT = 40 << 20


def whole(memory_space=pltpu.VMEM):
    return pl.BlockSpec(memory_space=memory_space)


def same_kernel(tokens, w_same, out):
    out[...] = jnp.dot(tokens[...], w_same[...], preferred_element_type=F32)


def same_product(tokens, w_same):
    rows, width = tokens.shape
    features = w_same.shape[1]
    tile = 512 if features % 512 == 0 else features
    return pl.pallas_call(
        same_kernel,
        grid=(features // tile,),
        in_specs=[
            pl.BlockSpec((rows, width), lambda i: (0, 0)),
            pl.BlockSpec((width, tile), lambda i: (0, i)),
        ],
        out_specs=pl.BlockSpec((rows, tile), lambda i: (0, i)),
        out_shape=jax.ShapeDtypeStruct((rows, features), F32),
        compiler_params=pltpu.CompilerParams(vmem_limit_bytes=16 << 20),
        cost_estimate=pl.CostEstimate(
            flops=2 * rows * width * features,
            bytes_accessed=2 * width * features + 6 * rows * features,
            transcendentals=0,
        ),
        name="same_product",
    )(tokens, w_same)


def reversed_rows(block):
    rows = block.shape[0]
    row = lax.broadcasted_iota(jnp.int32, (rows, rows), 0)
    column = lax.broadcasted_iota(jnp.int32, (rows, rows), 1)
    swap = (row + column == rows - 1).astype(F32).astype(BF16)
    return jnp.dot(swap, block, preferred_element_type=F32).astype(BF16)


def pack(pair, value, rows, lanes):
    width = value.shape[1]
    at = rows
    for lane in range(0, width - width % lanes, lanes):
        pair[at : at + rows, :] = value[:, lane : lane + lanes]
        at += rows
    rest = width % lanes
    if rest:
        share = rows * rest // lanes
        pair[at : at + share, :] = jnp.concatenate(
            [value[i * share : (i + 1) * share, width - rest :] for i in range(lanes // rest)], 1
        )


def unpack(pair, at, rows, lanes, width):
    key = pair[at : at + rows, :]
    at += rows
    parts = []
    for _ in range(width // lanes):
        parts.append(pair[at : at + rows, :])
        at += rows
    rest = width % lanes
    if rest:
        share = rows * rest // lanes
        tail = pair[at : at + share, :]
        parts.append(
            jnp.concatenate([tail[:, i * rest : (i + 1) * rest] for i in range(lanes // rest)], 0)
        )
    return key, jnp.concatenate(parts, 1)


def project_kernel(first, arrived, same, w_partner, w_query, w_key, w_value, query, pair):
    rows = arrived.shape[0]
    keys = w_key.shape[1]
    mirrored = reversed_rows(arrived[...])
    hidden = (
        same[first : first + rows, :] + jnp.dot(mirrored, w_partner[...], preferred_element_type=F32)
    ).astype(BF16)
    pair[:rows, :] = jnp.dot(hidden, w_key[...], preferred_element_type=F32).astype(BF16)
    value = lax.dot_general(
        hidden, w_value[...], CONTRACT_LAST, preferred_element_type=F32
    ).astype(BF16)
    pack(pair, value, rows, keys)
    query[...] = jnp.dot(hidden, w_query[...], preferred_element_type=F32).astype(BF16)


def project(first, arrived, same, w_partner, w_query, w_key, w_value):
    rows, width = arrived.shape
    queries, keys, values = w_query.shape[1], w_key.shape[1], w_value.shape[0]
    total = queries + keys + values
    return pl.pallas_call(
        functools.partial(project_kernel, first),
        in_specs=[whole()] * 6,
        out_specs=[whole()] * 2,
        out_shape=[
            jax.ShapeDtypeStruct((rows, queries), BF16),
            jax.ShapeDtypeStruct((rows * (keys + values) // keys, keys), BF16),
        ],
        compiler_params=pltpu.CompilerParams(vmem_limit_bytes=VMEM_LIMIT),
        cost_estimate=pl.CostEstimate(
            flops=2 * rows * width * (width + total),
            bytes_accessed=2 * width * (width + total),
            transcendentals=0,
        ),
        name="project",
    )(arrived, same, w_partner, w_query, w_key, w_value)


def attend_kernel(shape, *refs):
    n_query, blocks, has_state, last, heads, keys, values = shape
    refs = list(refs)
    queries = [refs.pop(0) for _ in range(n_query)]
    pairs = [refs.pop(0) for _ in blocks]
    if has_state:
        old_sum, old_peak = refs.pop(0), refs.pop(0)
    if last:
        w_out, out = refs.pop(0), refs.pop(0)
    else:
        new_sum, new_peak = refs.pop(0), refs.pop(0)
    held, extended, scores = refs.pop(0), refs.pop(0), refs.pop(0)
    if last:
        mixed = refs.pop(0)
    padded = extended.shape[1]
    scale = keys**-0.5 * math.log2(math.e)
    start = 0
    for pair, block in zip(pairs, blocks):
        packed = block * (keys + values) // keys
        for at in range(0, pair.shape[0], packed):
            key, value = unpack(pair, at, block, keys, values)
            held[start : start + block, :] = key
            extended[start : start + block, :values] = value
            start += block
    extended[:, values:] = jnp.ones((start, padded - values), BF16)
    step = 512 if start % 512 == 0 else 256

    def score(head, slot):
        column = pl.ds(pl.multiple_of(head * keys, keys), keys)
        parts = [query[:, column] for query in queries]
        query = jnp.concatenate(parts, 0) if len(parts) > 1 else parts[0]
        peak = None
        for at in range(0, start, step):
            block = lax.dot_general(
                query, held[at : at + step, :], CONTRACT_LAST, preferred_element_type=F32
            )
            scores[slot, :, at : at + step] = block
            for lane in range(0, step, 128):
                part = block[:, lane : lane + 128]
                peak = part if peak is None else jnp.maximum(peak, part)
        peak = jnp.max(peak, axis=1, keepdims=True)
        if has_state:
            peak = jnp.maximum(peak, old_peak[head][:, :1])
        return peak

    def mix(head, slot, peak):
        total = None
        for at in range(0, start, step):
            weights = jnp.exp2((scores[slot, :, at : at + step] - peak) * scale).astype(BF16)
            part = jnp.dot(weights, extended[at : at + step, :], preferred_element_type=F32)
            total = part if total is None else total + part
        if has_state:
            decay = jnp.exp2((old_peak[head][:, :1] - peak) * scale)
            total = total + old_sum[head] * decay
        if last:
            return (total[:, :values] / total[:, values : values + 1]).astype(BF16)
        new_sum[head] = total
        new_peak[head] = jnp.broadcast_to(peak, new_peak.shape[1:])
        return None

    def two_heads(index, peak):
        head = 2 * index
        other = score(head + 1, 1)
        left = mix(head, 0, peak)
        following = score(jnp.minimum(head + 2, heads - 1), 0)
        right = mix(head + 1, 1, other)
        if last:
            column = pl.ds(pl.multiple_of(index * 2 * values, 2 * values), 2 * values)
            mixed[:, column] = jnp.concatenate([left, right], 1)
        return following

    lax.fori_loop(0, heads // 2, two_heads, score(0, 0))
    if last:
        out[...] = jnp.dot(mixed[...], w_out[...], preferred_element_type=F32).astype(BF16)


def attend(queries, pairs, blocks, state, w_out, keys, values):
    rows = sum(query.shape[0] for query in queries)
    heads = queries[0].shape[1] // keys
    seen = sum(pair.shape[0] for pair in pairs) * keys // (keys + values)
    padded = (values // 128 + 1) * 128
    last = w_out is not None
    shape = (len(queries), blocks, state is not None, last, heads, keys, values)
    arguments = list(queries) + list(pairs) + (list(state) if state is not None else [])
    scratch = [pltpu.VMEM((seen, keys), BF16), pltpu.VMEM((seen, padded), BF16), pltpu.VMEM((2, rows, seen), F32)]
    if last:
        arguments.append(w_out)
        out_shape = jax.ShapeDtypeStruct((rows, w_out.shape[1]), BF16)
        out_specs = whole()
        scratch.append(pltpu.VMEM((rows, heads * values), BF16))
    else:
        out_shape = [
            jax.ShapeDtypeStruct((heads, rows, padded), F32),
            jax.ShapeDtypeStruct((heads, rows, 128), F32),
        ]
        out_specs = [whole()] * 2
    flops = 2 * rows * heads * seen * (keys + values)
    if last:
        flops += 2 * rows * heads * values * w_out.shape[1]
    return pl.pallas_call(
        functools.partial(attend_kernel, shape),
        in_specs=[whole()] * len(arguments),
        out_specs=out_specs,
        out_shape=out_shape,
        scratch_shapes=scratch,
        compiler_params=pltpu.CompilerParams(vmem_limit_bytes=VMEM_LIMIT),
        cost_estimate=pl.CostEstimate(
            flops=flops, bytes_accessed=2 * seen * (keys + values), transcendentals=rows * heads * seen
        ),
        name="attend",
    )(*arguments)


def gathered(pair):
    count = lax.axis_size("seq")
    parts = [pair] + [
        lax.ppermute(pair, "seq", [(s, s ^ k) for s in range(count)]) for k in range(2, count, 2)
    ]
    mine = jnp.concatenate(parts, 0)
    other = lax.ppermute(mine, "seq", [(s, s ^ 1) for s in range(count)])
    return [mine, other]


def body(tokens, w_same, w_partner, w_query, w_key, w_value, w_out):
    lanes, count = lax.axis_size("ws"), lax.axis_size("seq")
    local = tokens[0]
    rows = local.shape[0]
    keys, values = w_key.shape[1], w_value.shape[1]
    opposite = [
        (w * count + s, (w ^ 1) * count + count - 1 - s) for w in range(lanes) for s in range(count)
    ]
    sizes = [rows * part // sum(CHUNKS) for part in CHUNKS]
    starts = [sum(sizes[:i]) for i in range(len(sizes))]
    arrived = [
        lax.ppermute(local[rows - a - n : rows - a], ("ws", "seq"), opposite) if n < rows
        else lax.ppermute(local, ("ws", "seq"), opposite)
        for a, n in zip(starts, sizes)
    ]
    same = same_product(local, w_same)
    queries, pairs = [], []
    for a, block in zip(starts, arrived):
        query, pair = project(a, block, same, w_partner, w_query, w_key, w_value.T)
        queries.append(query)
        pairs.append(gathered(pair))
    state = None
    for index, (pair, size) in enumerate(zip(pairs, sizes)):
        final = w_out if index == len(pairs) - 1 else None
        state = attend(queries, pair, [size] * len(pair), state, final, keys, values)
    result = state
    return result[None]


def solution(mesh):
    placed = (P("ws", "seq", None), P(), P(), P(), P(), P(), P())
    return jax.shard_map(
        body, mesh=mesh, in_specs=placed, out_specs=P("ws", "seq", None), check_vma=False
    )
```

```python
import functools
import math

import jax
import jax.numpy as jnp
from jax import lax
from jax.experimental import pallas as pl
from jax.experimental.pallas import tpu as pltpu
from jax.sharding import PartitionSpec as P

F32 = jnp.float32
BF16 = jnp.bfloat16
CONTRACT_LAST = (((1,), (1,)), ((), ()))
STACKED = 384


def whole(memory_space=pltpu.VMEM):
    return pl.BlockSpec(memory_space=memory_space)


def reversed_rows(block):
    rows = block.shape[0]
    row = lax.broadcasted_iota(jnp.int32, (rows, rows), 0)
    column = lax.broadcasted_iota(jnp.int32, (rows, rows), 1)
    swap = (row + column == rows - 1).astype(F32).astype(BF16)
    return jnp.dot(swap, block, preferred_element_type=F32).astype(BF16)


def product(left, right):
    return jnp.dot(left, right, preferred_element_type=F32)


def own_kernel(tokens, w_same, w_partner, w_key, w_value, same, partner, w_pair):
    rows, keys = same.shape[0], w_key.shape[1]
    w_pair[:, :keys] = w_key[...]
    w_pair[:, keys : keys + w_value.shape[0]] = w_value[...].T
    w_pair[:, keys + w_value.shape[0] :] = jnp.zeros(
        (w_pair.shape[0], w_pair.shape[1] - keys - w_value.shape[0]), BF16
    )
    block = tokens[:rows, :]
    same[...] = product(block, w_same[...])
    partner[...] = product(reversed_rows(block), w_partner[...])


def own_products(tokens, w_same, w_partner, w_key, w_value, rows):
    width, features = w_same.shape
    both = -(-(w_key.shape[1] + w_value.shape[0]) // 128) * 128
    return pl.pallas_call(
        own_kernel,
        in_specs=[whole()] * 5,
        out_specs=[whole()] * 3,
        out_shape=[jax.ShapeDtypeStruct((rows, features), F32)] * 2
        + [jax.ShapeDtypeStruct((width, both), BF16)],
        compiler_params=pltpu.CompilerParams(vmem_limit_bytes=20 << 20),
        cost_estimate=pl.CostEstimate(
            flops=4 * rows * width * features, bytes_accessed=4 * width * features, transcendentals=0
        ),
        name="own_products",
    )(tokens, w_same, w_partner, w_key, w_value)


def pack(pair, value, rows, lanes):
    width = value.shape[1]
    at = rows
    for lane in range(0, width - width % lanes, lanes):
        pair[at : at + rows, :] = value[:, lane : lane + lanes]
        at += rows
    rest = width % lanes
    if rest:
        share = rows * rest // lanes
        pair[at : at + share, :] = jnp.concatenate(
            [value[i * share : (i + 1) * share, width - rest :] for i in range(lanes // rest)], 1
        )


def unpack(pair, at, rows, lanes, width):
    key = pair[at : at + rows, :]
    at += rows
    parts = []
    for _ in range(width // lanes):
        parts.append(pair[at : at + rows, :])
        at += rows
    rest = width % lanes
    if rest:
        share = rows * rest // lanes
        tail = pair[at : at + share, :]
        parts.append(
            jnp.concatenate([tail[:, i * rest : (i + 1) * rest] for i in range(lanes // rest)], 0)
        )
    return key, jnp.concatenate(parts, 1)


def hidden_kernel(keys, values, arrived, same, partner, w_same, w_partner, w_pair, hidden, own, other):
    rows = arrived.shape[0]
    block = arrived[...]
    upper = (same[...] + product(reversed_rows(block), w_partner[...])).astype(BF16)
    lower = (product(block, w_same[...]) + partner[...]).astype(BF16)
    hidden[:rows, :] = upper
    hidden[rows:, :] = lower
    both = jnp.concatenate([upper, lower], 0)
    result = product(both, w_pair[...]).astype(BF16)
    for pair, at in ((own, 0), (other, rows)):
        pair[:rows, :] = result[at : at + rows, :keys]
        pack(pair, result[at : at + rows, keys : keys + values], rows, keys)


def hidden_and_pairs(arrived, same, partner, w_same, w_partner, w_pair, keys, values):
    rows, width = arrived.shape
    pair = jax.ShapeDtypeStruct((rows * (keys + values) // keys, keys), BF16)
    return pl.pallas_call(
        functools.partial(hidden_kernel, keys, values),
        in_specs=[whole()] * 6,
        out_specs=[whole()] * 3,
        out_shape=[jax.ShapeDtypeStruct((2 * rows, width), BF16), pair, pair],
        compiler_params=pltpu.CompilerParams(vmem_limit_bytes=20 << 20),
        cost_estimate=pl.CostEstimate(
            flops=4 * rows * width * (width + keys + values),
            bytes_accessed=4 * width * width,
            transcendentals=0,
        ),
        name="hidden_and_pairs",
    )(arrived, same, partner, w_same, w_partner, w_pair)


def query_kernel(hidden, w_query, *queries):
    result = product(hidden[...], w_query[...]).astype(BF16)
    at = 0
    for query in queries:
        query[...] = result[at : at + query.shape[0], :]
        at += query.shape[0]


def query_rows(hidden, w_query, sizes):
    width, queries = w_query.shape
    return pl.pallas_call(
        query_kernel,
        in_specs=[whole()] * 2,
        out_specs=[whole()] * len(sizes),
        out_shape=[jax.ShapeDtypeStruct((size, queries), BF16) for size in sizes],
        compiler_params=pltpu.CompilerParams(vmem_limit_bytes=16 << 20),
        cost_estimate=pl.CostEstimate(
            flops=2 * hidden.shape[0] * width * queries,
            bytes_accessed=2 * width * queries,
            transcendentals=0,
        ),
        name="query_rows",
    )(hidden, w_query)


def attend_kernel(shape, *refs):
    n_query, blocks, has_state, last, heads, group, keys, values = shape
    refs = list(refs)
    queries = [refs.pop(0) for _ in range(n_query)]
    pairs = [refs.pop(0) for _ in blocks]
    states = [(refs.pop(0), refs.pop(0)) for _ in range(n_query if has_state else 0)]
    if last:
        w_out, out = refs.pop(0), refs.pop(0)
    else:
        new_sum, new_peak = refs.pop(0), refs.pop(0)
    held, extended, scores = refs.pop(0), refs.pop(0), refs.pop(0)
    if last:
        mixed = refs.pop(0)
    rows = queries[0].shape[0]
    units = [(index, unit) for index in range(n_query) for unit in range(heads // group)]
    padded = extended.shape[1]
    scale = keys**-0.5 * math.log2(math.e)
    seen = 0
    for pair, block in zip(pairs, blocks):
        packed = block * (keys + values) // keys
        for at in range(0, pair.shape[0], packed):
            key, value = unpack(pair, at, block, keys, values)
            held[seen : seen + block, :] = key
            extended[seen : seen + block, :values] = value
            seen += block
    extended[:, values:] = jnp.ones((seen, padded - values), BF16)
    step = 512 if seen % 512 == 0 else 256

    def score(index, unit, slot):
        wide = group * keys
        columns = queries[index][:, unit * wide : (unit + 1) * wide]
        stacked = jnp.concatenate([columns[:, i * keys : (i + 1) * keys] for i in range(group)], 0)
        peak = None
        for at in range(0, seen, step):
            block = lax.dot_general(
                stacked, held[at : at + step, :], CONTRACT_LAST, preferred_element_type=F32
            )
            scores[slot, :, at : at + step] = block
            for lane in range(0, step, 128):
                part = block[:, lane : lane + 128]
                peak = part if peak is None else jnp.maximum(peak, part)
        peak = jnp.max(peak, axis=1, keepdims=True)
        if has_state:
            peak = jnp.maximum(peak, states[index][1][unit][:, :1])
        return peak

    def mix(index, unit, slot, peak):
        total = None
        for at in range(0, seen, step):
            weights = jnp.exp2((scores[slot, :, at : at + step] - peak) * scale).astype(BF16)
            part = jnp.dot(weights, extended[at : at + step, :], preferred_element_type=F32)
            total = part if total is None else total + part
        if has_state:
            old_sum, old_peak = states[index]
            decay = jnp.exp2((old_peak[unit][:, :1] - peak) * scale)
            total = total + old_sum[unit] * decay
        if not last:
            new_sum[unit] = total
            new_peak[unit] = jnp.broadcast_to(peak, new_peak.shape[1:])
            return
        result = (total[:, :values] / total[:, values : values + 1]).astype(BF16)
        wide = group * values
        mixed[index * rows : (index + 1) * rows, unit * wide : (unit + 1) * wide] = jnp.concatenate(
            [result[i * rows : (i + 1) * rows, :] for i in range(group)], 1
        )

    peak = score(*units[0], 0)
    for at, unit in enumerate(units):
        following = score(*units[at + 1], (at + 1) % 2) if at + 1 < len(units) else None
        mix(*unit, at % 2, peak)
        peak = following
    if last:
        out[...] = product(mixed[...], w_out[...]).astype(BF16)


def attend(queries, pairs, block, keys, values, states=None, w_out=None, weight=1.0):
    rows = queries[0].shape[0]
    heads = queries[0].shape[1] // keys
    group = 2
    while group * rows < STACKED and heads % (2 * group) == 0:
        group *= 2
    seen = sum(pair.shape[0] for pair in pairs) * keys // (keys + values)
    padded = (values // 128 + 1) * 128
    last = w_out is not None
    shape = (len(queries), [block] * len(pairs), states is not None, last, heads, group, keys, values)
    arguments = list(queries) + list(pairs) + [part for state in states or () for part in state]
    scratch = [
        pltpu.VMEM((seen, keys), BF16),
        pltpu.VMEM((seen, padded), BF16),
        pltpu.VMEM((2, group * rows, seen), F32),
    ]
    if last:
        arguments.append(w_out)
        out_shape = jax.ShapeDtypeStruct((rows * len(queries), w_out.shape[1]), BF16)
        out_specs = whole()
        scratch.append(pltpu.VMEM((rows * len(queries), heads * values), BF16))
    else:
        out_shape = [
            jax.ShapeDtypeStruct((heads // group, group * rows, padded), F32),
            jax.ShapeDtypeStruct((heads // group, group * rows, 128), F32),
        ]
        out_specs = [whole()] * 2
    flops = int(weight * 2 * len(queries) * rows * heads * seen * (keys + values))
    if last:
        flops += 2 * len(queries) * rows * heads * values * w_out.shape[1]
    return pl.pallas_call(
        functools.partial(attend_kernel, shape),
        in_specs=[whole()] * len(arguments),
        out_specs=out_specs,
        out_shape=out_shape,
        scratch_shapes=scratch,
        compiler_params=pltpu.CompilerParams(vmem_limit_bytes=28 << 20),
        cost_estimate=pl.CostEstimate(
            flops=flops,
            bytes_accessed=2 * seen * (keys + values),
            transcendentals=0,
        ),
        name="attend",
    )(*arguments)


def to_both_cores(parts):
    count = lax.axis_size("seq")
    return parts + [lax.ppermute(part, "seq", [(s, s ^ 1) for s in range(count)]) for part in parts]


def crossed(value, lane_bit, place_bits):
    lanes, count = lax.axis_size("ws"), lax.axis_size("seq")
    pairs = [
        (w * count + s, (w ^ lane_bit) * count + (s ^ place_bits))
        for w in range(lanes)
        for s in range(count)
    ]
    return lax.ppermute(value, ("ws", "seq"), pairs)


def body(tokens, w_same, w_partner, w_query, w_key, w_value, w_out):
    count = lax.axis_size("seq")
    local = tokens[0]
    half = local.shape[0] // 2
    keys, values = w_key.shape[1], w_value.shape[1]
    arrived = crossed(local[half:], 1, count - 1)
    same, partner, w_pair = own_products(local, w_same, w_partner, w_key, w_value.T, half)
    hidden, own, other = hidden_and_pairs(
        arrived, same, partner, w_same, w_partner, w_pair, keys, values
    )
    near = [own] + [crossed(own, 0, k) for k in range(2, count, 2)]
    lifted = crossed(other, 1, 0)
    query, sent = query_rows(hidden, w_query, [half, half])
    near, lifted, query = lax.optimization_barrier((near, lifted, query))
    near = to_both_cores(near)
    brought = crossed(sent, 1, count - 1)
    mine = attend([query], near, half, keys, values, weight=1.7)
    brought, mine = lax.optimization_barrier((brought, mine))
    far = [lifted] + [crossed(lifted, 0, k) for k in range(2, count, 2)]
    theirs = attend([brought], near, half, keys, values, weight=0.1)
    far, theirs = lax.optimization_barrier((far, theirs))
    far = to_both_cores(far)
    result = attend([query, brought], far, half, keys, values, [mine, theirs], w_out)
    return result[None]


def solution(mesh):
    placed = (P("ws", "seq", None), P(), P(), P(), P(), P(), P())
    return jax.shard_map(
        body, mesh=mesh, in_specs=placed, out_specs=P("ws", "seq", None), check_vma=False
    )
```

```python
import functools
import math

import jax
import jax.numpy as jnp
from jax import lax
from jax.experimental import pallas as pl
from jax.experimental.pallas import tpu as pltpu
from jax.sharding import PartitionSpec as P

F32 = jnp.float32
BF16 = jnp.bfloat16
CONTRACT_LAST = (((1,), (1,)), ((), ()))
STACKED = 384
COLUMNS = (2, 1)


def whole(memory_space=pltpu.VMEM):
    return pl.BlockSpec(memory_space=memory_space)


def reversed_rows(block):
    rows = block.shape[0]
    row = lax.broadcasted_iota(jnp.int32, (rows, rows), 0)
    column = lax.broadcasted_iota(jnp.int32, (rows, rows), 1)
    swap = (row + column == rows - 1).astype(F32).astype(BF16)
    return jnp.dot(swap, block, preferred_element_type=F32).astype(BF16)


def product(left, right):
    return jnp.dot(left, right, preferred_element_type=F32)


def own_kernel(tokens, w_same, w_partner, w_key, w_value, same, partner, w_pair):
    rows, keys = same.shape[0], w_key.shape[1]
    w_pair[:, :keys] = w_key[...]
    w_pair[:, keys : keys + w_value.shape[0]] = w_value[...].T
    w_pair[:, keys + w_value.shape[0] :] = jnp.zeros(
        (w_pair.shape[0], w_pair.shape[1] - keys - w_value.shape[0]), BF16
    )
    block = tokens[:rows, :]
    same[...] = product(block, w_same[...])
    partner[...] = product(reversed_rows(block), w_partner[...])


def own_products(tokens, w_same, w_partner, w_key, w_value, rows):
    width, features = w_same.shape
    both = -(-(w_key.shape[1] + w_value.shape[0]) // 128) * 128
    return pl.pallas_call(
        own_kernel,
        in_specs=[whole()] * 5,
        out_specs=[whole()] * 3,
        out_shape=[jax.ShapeDtypeStruct((rows, features), F32)] * 2
        + [jax.ShapeDtypeStruct((width, both), BF16)],
        compiler_params=pltpu.CompilerParams(vmem_limit_bytes=20 << 20),
        cost_estimate=pl.CostEstimate(
            flops=4 * rows * width * features, bytes_accessed=4 * width * features, transcendentals=0
        ),
        name="own_products",
    )(tokens, w_same, w_partner, w_key, w_value)


def pack(pair, value, rows, lanes):
    width = value.shape[1]
    at = rows
    for lane in range(0, width - width % lanes, lanes):
        pair[at : at + rows, :] = value[:, lane : lane + lanes]
        at += rows
    rest = width % lanes
    if rest:
        share = rows * rest // lanes
        pair[at : at + share, :] = jnp.concatenate(
            [value[i * share : (i + 1) * share, width - rest :] for i in range(lanes // rest)], 1
        )


def unpack(pair, at, rows, lanes, width):
    key = pair[at : at + rows, :]
    at += rows
    parts = []
    for _ in range(width // lanes):
        parts.append(pair[at : at + rows, :])
        at += rows
    rest = width % lanes
    if rest:
        share = rows * rest // lanes
        tail = pair[at : at + share, :]
        parts.append(
            jnp.concatenate([tail[:, i * rest : (i + 1) * rest] for i in range(lanes // rest)], 0)
        )
    return key, jnp.concatenate(parts, 1)


def add_kernel(at, arrived, same, partner, w_same, w_partner, upper, lower):
    block = arrived[...]
    depth = pl.ds(at, block.shape[1])
    upper[...] = same[...] + product(reversed_rows(block), w_partner[depth, :])
    lower[...] = partner[...] + product(block, w_same[depth, :])


def add_products(at, arrived, same, partner, w_same, w_partner):
    rows, width = arrived.shape
    features = w_same.shape[1]
    return pl.pallas_call(
        functools.partial(add_kernel, at),
        in_specs=[whole()] * 5,
        out_specs=[whole()] * 2,
        out_shape=[jax.ShapeDtypeStruct((rows, features), F32)] * 2,
        compiler_params=pltpu.CompilerParams(vmem_limit_bytes=20 << 20),
        cost_estimate=pl.CostEstimate(
            flops=4 * rows * width * features, bytes_accessed=4 * width * features, transcendentals=0
        ),
        name="add_products",
    )(arrived, same, partner, w_same, w_partner)


def hidden_kernel(keys, values, at, arrived, same, partner, w_same, w_partner, w_pair, hidden, own, other):
    rows = arrived.shape[0]
    block = arrived[...]
    depth = pl.ds(at, block.shape[1])
    upper = (same[...] + product(reversed_rows(block), w_partner[depth, :])).astype(BF16)
    lower = (partner[...] + product(block, w_same[depth, :])).astype(BF16)
    hidden[:rows, :] = upper
    hidden[rows:, :] = lower
    both = jnp.concatenate([upper, lower], 0)
    result = product(both, w_pair[...]).astype(BF16)
    for pair, first in ((own, 0), (other, rows)):
        pair[:rows, :] = result[first : first + rows, :keys]
        pack(pair, result[first : first + rows, keys : keys + values], rows, keys)


def hidden_and_pairs(at, arrived, same, partner, w_same, w_partner, w_pair, keys, values):
    rows, width = arrived.shape
    features = w_same.shape[1]
    pair = jax.ShapeDtypeStruct((rows * (keys + values) // keys, keys), BF16)
    return pl.pallas_call(
        functools.partial(hidden_kernel, keys, values, at),
        in_specs=[whole()] * 6,
        out_specs=[whole()] * 3,
        out_shape=[jax.ShapeDtypeStruct((2 * rows, features), BF16), pair, pair],
        compiler_params=pltpu.CompilerParams(vmem_limit_bytes=20 << 20),
        cost_estimate=pl.CostEstimate(
            flops=4 * rows * (width * features + features * (keys + values)),
            bytes_accessed=4 * width * features,
            transcendentals=0,
        ),
        name="hidden_and_pairs",
    )(arrived, same, partner, w_same, w_partner, w_pair)


def query_kernel(hidden, w_query, *queries):
    result = product(hidden[...], w_query[...]).astype(BF16)
    at = 0
    for query in queries:
        query[...] = result[at : at + query.shape[0], :]
        at += query.shape[0]


def query_rows(hidden, w_query, sizes):
    width, queries = w_query.shape
    return pl.pallas_call(
        query_kernel,
        in_specs=[whole()] * 2,
        out_specs=[whole()] * len(sizes),
        out_shape=[jax.ShapeDtypeStruct((size, queries), BF16) for size in sizes],
        compiler_params=pltpu.CompilerParams(vmem_limit_bytes=16 << 20),
        cost_estimate=pl.CostEstimate(
            flops=2 * hidden.shape[0] * width * queries,
            bytes_accessed=2 * width * queries,
            transcendentals=0,
        ),
        name="query_rows",
    )(hidden, w_query)


def attend_kernel(shape, *refs):
    n_query, blocks, has_state, last, carried, heads, group, keys, values = shape
    refs = list(refs)
    queries = [refs.pop(0) for _ in range(n_query)]
    pairs = [refs.pop(0) for _ in blocks]
    states = [(refs.pop(0), refs.pop(0)) for _ in range(n_query if has_state else 0)]
    if last:
        w_out = refs.pop(0)
        if carried:
            refs.pop(0)
        out = refs.pop(0)
    else:
        new_sum, new_peak = refs.pop(0), refs.pop(0)
    held, extended, scores = refs.pop(0), refs.pop(0), refs.pop(0)
    if last:
        mixed = refs.pop(0)
    rows = queries[0].shape[0]
    units = [(index, unit) for index in range(n_query) for unit in range(heads // group)]
    padded = extended.shape[1]
    scale = keys**-0.5 * math.log2(math.e)
    seen = 0
    for pair, block in zip(pairs, blocks):
        packed = block * (keys + values) // keys
        for at in range(0, pair.shape[0], packed):
            key, value = unpack(pair, at, block, keys, values)
            held[seen : seen + block, :] = key
            extended[seen : seen + block, :values] = value
            seen += block
    extended[:, values:] = jnp.ones((seen, padded - values), BF16)
    steps = [(at, min(512, seen - at)) for at in range(0, seen, 512)]

    def score(index, unit, slot):
        wide = group * keys
        columns = queries[index][:, unit * wide : (unit + 1) * wide]
        stacked = jnp.concatenate([columns[:, i * keys : (i + 1) * keys] for i in range(group)], 0)
        peak = None
        for at, step in steps:
            block = lax.dot_general(
                stacked, held[at : at + step, :], CONTRACT_LAST, preferred_element_type=F32
            )
            scores[slot, :, at : at + step] = block
            for lane in range(0, step, 128):
                part = block[:, lane : lane + 128]
                peak = part if peak is None else jnp.maximum(peak, part)
        peak = jnp.max(peak, axis=1, keepdims=True)
        if has_state:
            peak = jnp.maximum(peak, states[index][1][unit][:, :1])
        return peak

    def mix(index, unit, slot, peak):
        total = None
        for at, step in steps:
            weights = jnp.exp2((scores[slot, :, at : at + step] - peak) * scale).astype(BF16)
            part = jnp.dot(weights, extended[at : at + step, :], preferred_element_type=F32)
            total = part if total is None else total + part
        if has_state:
            old_sum, old_peak = states[index]
            decay = jnp.exp2((old_peak[unit][:, :1] - peak) * scale)
            total = total + old_sum[unit] * decay
        if not last:
            new_sum[unit] = total
            new_peak[unit] = jnp.broadcast_to(peak, new_peak.shape[1:])
            return
        result = (total[:, :values] / total[:, values : values + 1]).astype(BF16)
        wide = group * values
        mixed[index * rows : (index + 1) * rows, unit * wide : (unit + 1) * wide] = jnp.concatenate(
            [result[i * rows : (i + 1) * rows, :] for i in range(group)], 1
        )

    peak = score(*units[0], 0)
    for at, unit in enumerate(units):
        following = score(*units[at + 1], (at + 1) % 2) if at + 1 < len(units) else None
        mix(*unit, at % 2, peak)
        peak = following
    if last:
        out[...] = product(mixed[...], w_out[...]).astype(BF16)


def attend(queries, pairs, block, keys, values, states=None, w_out=None, place=None, carried=None, weight=1.0):
    rows = queries[0].shape[0]
    heads = queries[0].shape[1] // keys
    group = 2
    while group * rows < STACKED and heads % (2 * group) == 0:
        group *= 2
    seen = sum(pair.shape[0] for pair in pairs) * keys // (keys + values)
    padded = (values // 128 + 1) * 128
    last = w_out is not None
    shape = (len(queries), [block] * len(pairs), states is not None, last, carried is not None, heads, group, keys, values)
    arguments = list(queries) + list(pairs) + [part for state in states or () for part in state]
    scratch = [
        pltpu.VMEM((seen, keys), BF16),
        pltpu.VMEM((seen, padded), BF16),
        pltpu.VMEM((2, group * rows, seen), F32),
    ]
    in_specs = [whole()] * len(arguments)
    aliases = {}
    if last:
        index, count = place
        arguments.append(w_out)
        in_specs.append(whole())
        if carried is not None:
            aliases = {len(arguments): 0}
            arguments.append(carried)
            in_specs.append(whole(pl.ANY))
        out_shape = jax.ShapeDtypeStruct((rows * len(queries) * count, w_out.shape[1]), BF16)
        out_specs = pl.BlockSpec((rows * len(queries), w_out.shape[1]), lambda i: (index, 0))
        scratch.append(pltpu.VMEM((rows * len(queries), heads * values), BF16))
    else:
        out_shape = [
            jax.ShapeDtypeStruct((heads // group, group * rows, padded), F32),
            jax.ShapeDtypeStruct((heads // group, group * rows, 128), F32),
        ]
        out_specs = [whole()] * 2
    flops = int(weight * 2 * len(queries) * rows * heads * seen * (keys + values))
    if last:
        flops += 2 * len(queries) * rows * heads * values * w_out.shape[1]
    return pl.pallas_call(
        functools.partial(attend_kernel, shape),
        grid=(1,),
        in_specs=in_specs,
        out_specs=out_specs,
        out_shape=out_shape,
        scratch_shapes=scratch,
        input_output_aliases=aliases,
        compiler_params=pltpu.CompilerParams(vmem_limit_bytes=28 << 20),
        cost_estimate=pl.CostEstimate(
            flops=flops,
            bytes_accessed=2 * seen * (keys + values),
            transcendentals=0,
        ),
        name="attend",
    )(*arguments)


def other_core(value):
    count = lax.axis_size("seq")
    return lax.ppermute(value, "seq", [(s, s ^ 1) for s in range(count)])


def after(value, *others):
    return lax.optimization_barrier((value, *others))[0]


def crossed(value, lane_bit, place_bits):
    lanes, count = lax.axis_size("ws"), lax.axis_size("seq")
    bits = place_bits if isinstance(place_bits, tuple) else (place_bits, place_bits)
    pairs = [
        (w * count + s, (w ^ lane_bit) * count + (s ^ bits[s % 2]))
        for w in range(lanes)
        for s in range(count)
    ]
    return lax.ppermute(value, ("ws", "seq"), pairs)


def spread(block, twin):
    places = list(range(2, lax.axis_size("seq"), 2))
    whole_chip = jnp.concatenate([block, twin], 0)
    single = crossed(block, 0, places[-1])
    return [single] + [
        crossed(whole_chip, 0, (places[i], places[i + 1])) for i in range(0, len(places) - 1, 2)
    ]


def body(tokens, w_same, w_partner, w_query, w_key, w_value, w_out):
    count = lax.axis_size("seq")
    local = tokens[0]
    half = local.shape[0] // 2
    keys, values = w_key.shape[1], w_value.shape[1]
    width = local.shape[1]
    sizes = [width * part // sum(COLUMNS) for part in COLUMNS]
    spans = [(sum(sizes[:i]), size) for i, size in enumerate(sizes)]
    arrived = [crossed(piece, 1, count - 1) for piece in [local[half:, at : at + size] for at, size in spans]]
    same, partner, w_pair = own_products(local, w_same, w_partner, w_key, w_value.T, half)
    for (at, _), piece in zip(spans[:-1], arrived[:-1]):
        same, partner = add_products(at, piece, same, partner, w_same, w_partner)
    hidden, own, other = hidden_and_pairs(
        spans[-1][0], arrived[-1], same, partner, w_same, w_partner, w_pair, keys, values
    )
    places = range(2, count, 2)
    near = [own] + [crossed(own, 0, k) for k in places]
    lifted = crossed(other, 1, 0)
    query, sent = query_rows(hidden, w_query, [half, half])
    near, lifted, query = lax.optimization_barrier((near, lifted, query))
    high = other_core(lifted)
    early = near + [other_core(part) for part in near] + [lifted, high]
    brought = crossed(sent, 1, count - 1)
    mine = attend([query], early, half, keys, values, weight=0.7)
    brought = after(brought, mine)
    far = spread(lifted, high)
    theirs = attend([brought], early, half, keys, values, weight=1.0)
    far = after(far, theirs)
    late = far + [other_core(part) for part in far]
    result = attend([query, brought], late, half, keys, values, [mine, theirs], w_out, (0, 1))
    return result[None]


def solution(mesh):
    placed = (P("ws", "seq", None), P(), P(), P(), P(), P(), P())
    return jax.shard_map(
        body, mesh=mesh, in_specs=placed, out_specs=P("ws", "seq", None), check_vma=False
    )
```

```python
import functools
import math

import jax
import jax.numpy as jnp
from jax import lax
from jax.experimental import pallas as pl
from jax.experimental.pallas import tpu as pltpu
from jax.sharding import PartitionSpec as P

F32 = jnp.float32
BF16 = jnp.bfloat16
CONTRACT_LAST = (((1,), (1,)), ((), ()))
STACKED = 384
COLUMNS = (5, 1)


def whole(memory_space=pltpu.VMEM):
    return pl.BlockSpec(memory_space=memory_space)


def reversed_rows(block):
    rows = block.shape[0]
    row = lax.broadcasted_iota(jnp.int32, (rows, rows), 0)
    column = lax.broadcasted_iota(jnp.int32, (rows, rows), 1)
    swap = (row + column == rows - 1).astype(F32).astype(BF16)
    return jnp.dot(swap, block, preferred_element_type=F32).astype(BF16)


def product(left, right):
    return jnp.dot(left, right, preferred_element_type=F32)


def own_kernel(tokens, w_same, w_partner, w_key, w_value, same, partner, w_pair):
    rows, keys = same.shape[0], w_key.shape[1]
    w_pair[:, :keys] = w_key[...]
    w_pair[:, keys : keys + w_value.shape[0]] = w_value[...].T
    w_pair[:, keys + w_value.shape[0] :] = jnp.zeros(
        (w_pair.shape[0], w_pair.shape[1] - keys - w_value.shape[0]), BF16
    )
    block = tokens[:rows, :]
    same[...] = product(block, w_same[...])
    partner[...] = product(reversed_rows(block), w_partner[...])


def own_products(tokens, w_same, w_partner, w_key, w_value, rows):
    width, features = w_same.shape
    both = -(-(w_key.shape[1] + w_value.shape[0]) // 128) * 128
    return pl.pallas_call(
        own_kernel,
        in_specs=[whole()] * 5,
        out_specs=[whole()] * 3,
        out_shape=[jax.ShapeDtypeStruct((rows, features), F32)] * 2
        + [jax.ShapeDtypeStruct((width, both), BF16)],
        compiler_params=pltpu.CompilerParams(vmem_limit_bytes=20 << 20),
        cost_estimate=pl.CostEstimate(
            flops=4 * rows * width * features, bytes_accessed=4 * width * features, transcendentals=0
        ),
        name="own_products",
    )(tokens, w_same, w_partner, w_key, w_value)


def pack(pair, value, rows, lanes):
    width = value.shape[1]
    at = rows
    for lane in range(0, width - width % lanes, lanes):
        pair[at : at + rows, :] = value[:, lane : lane + lanes]
        at += rows
    rest = width % lanes
    if rest:
        share = rows * rest // lanes
        pair[at : at + share, :] = jnp.concatenate(
            [value[i * share : (i + 1) * share, width - rest :] for i in range(lanes // rest)], 1
        )


def unpack(pair, at, rows, lanes, width):
    key = pair[at : at + rows, :]
    at += rows
    parts = []
    for _ in range(width // lanes):
        parts.append(pair[at : at + rows, :])
        at += rows
    rest = width % lanes
    if rest:
        share = rows * rest // lanes
        tail = pair[at : at + share, :]
        parts.append(
            jnp.concatenate([tail[:, i * rest : (i + 1) * rest] for i in range(lanes // rest)], 0)
        )
    return key, jnp.concatenate(parts, 1)


def add_kernel(at, arrived, same, partner, w_same, w_partner, upper, lower):
    block = arrived[...]
    depth = pl.ds(at, block.shape[1])
    upper[...] = same[...] + product(reversed_rows(block), w_partner[depth, :])
    lower[...] = partner[...] + product(block, w_same[depth, :])


def add_products(at, arrived, same, partner, w_same, w_partner):
    rows, width = arrived.shape
    features = w_same.shape[1]
    return pl.pallas_call(
        functools.partial(add_kernel, at),
        in_specs=[whole()] * 5,
        out_specs=[whole()] * 2,
        out_shape=[jax.ShapeDtypeStruct((rows, features), F32)] * 2,
        compiler_params=pltpu.CompilerParams(vmem_limit_bytes=20 << 20),
        cost_estimate=pl.CostEstimate(
            flops=4 * rows * width * features, bytes_accessed=4 * width * features, transcendentals=0
        ),
        name="add_products",
    )(arrived, same, partner, w_same, w_partner)


def hidden_kernel(keys, values, at, arrived, same, partner, w_same, w_partner, w_pair, hidden, own, other):
    rows = arrived.shape[0]
    block = arrived[...]
    depth = pl.ds(at, block.shape[1])
    upper = (same[...] + product(reversed_rows(block), w_partner[depth, :])).astype(BF16)
    lower = (partner[...] + product(block, w_same[depth, :])).astype(BF16)
    hidden[:rows, :] = upper
    hidden[rows:, :] = lower
    both = jnp.concatenate([upper, lower], 0)
    result = product(both, w_pair[...]).astype(BF16)
    for pair, first in ((own, 0), (other, rows)):
        pair[:rows, :] = result[first : first + rows, :keys]
        pack(pair, result[first : first + rows, keys : keys + values], rows, keys)


def hidden_and_pairs(at, arrived, same, partner, w_same, w_partner, w_pair, keys, values):
    rows, width = arrived.shape
    features = w_same.shape[1]
    pair = jax.ShapeDtypeStruct((rows * (keys + values) // keys, keys), BF16)
    return pl.pallas_call(
        functools.partial(hidden_kernel, keys, values, at),
        in_specs=[whole()] * 6,
        out_specs=[whole()] * 3,
        out_shape=[jax.ShapeDtypeStruct((2 * rows, features), BF16), pair, pair],
        compiler_params=pltpu.CompilerParams(vmem_limit_bytes=20 << 20),
        cost_estimate=pl.CostEstimate(
            flops=4 * rows * (width * features + features * (keys + values)),
            bytes_accessed=4 * width * features,
            transcendentals=0,
        ),
        name="hidden_and_pairs",
    )(arrived, same, partner, w_same, w_partner, w_pair)


def query_kernel(hidden, w_query, *queries):
    result = product(hidden[...], w_query[...]).astype(BF16)
    at = 0
    for query in queries:
        query[...] = result[at : at + query.shape[0], :]
        at += query.shape[0]


def query_rows(hidden, w_query, sizes):
    width, queries = w_query.shape
    return pl.pallas_call(
        query_kernel,
        in_specs=[whole()] * 2,
        out_specs=[whole()] * len(sizes),
        out_shape=[jax.ShapeDtypeStruct((size, queries), BF16) for size in sizes],
        compiler_params=pltpu.CompilerParams(vmem_limit_bytes=16 << 20),
        cost_estimate=pl.CostEstimate(
            flops=2 * hidden.shape[0] * width * queries,
            bytes_accessed=2 * width * queries,
            transcendentals=0,
        ),
        name="query_rows",
    )(hidden, w_query)


def attend_kernel(shape, *refs):
    n_query, blocks, lead, drop, has_state, last, carried, heads, group, keys, values = shape
    refs = list(refs)
    queries = [refs.pop(0) for _ in range(n_query)]
    pairs = [refs.pop(0) for _ in blocks]
    states = [(refs.pop(0), refs.pop(0)) for _ in range(n_query if has_state else 0)]
    if last:
        w_out = refs.pop(0)
        if carried:
            refs.pop(0)
        out = refs.pop(0)
    else:
        new_sum, new_peak = refs.pop(0), refs.pop(0)
    held, extended, scores = refs.pop(0), refs.pop(0), refs.pop(0)
    if last:
        mixed = refs.pop(0)
    rows = queries[0].shape[0]
    units = [(index, unit) for index in range(n_query) for unit in range(heads // group)]
    padded = extended.shape[1]
    scale = keys**-0.5 * math.log2(math.e)
    seen = 0
    for pair, block in zip(pairs, blocks):
        packed = block * (keys + values) // keys
        for at in range(0, pair.shape[0], packed):
            key, value = unpack(pair, at, block, keys, values)
            taken = lead if lead and not seen else block
            held[seen : seen + taken, :] = key[block - taken :, :]
            extended[seen : seen + taken, :values] = value[block - taken :, :]
            seen += taken
    extended[:, values:] = jnp.ones((seen, padded - values), BF16)
    seen -= drop
    steps = [(at, min(512, seen - at)) for at in range(0, seen, 512)]

    def score(index, unit, slot):
        wide = group * keys
        columns = queries[index][:, unit * wide : (unit + 1) * wide]
        stacked = jnp.concatenate([columns[:, i * keys : (i + 1) * keys] for i in range(group)], 0)
        peak = None
        for at, step in steps:
            block = lax.dot_general(
                stacked, held[at : at + step, :], CONTRACT_LAST, preferred_element_type=F32
            )
            scores[slot, :, at : at + step] = block
            for lane in range(0, step, 128):
                part = block[:, lane : lane + 128]
                peak = part if peak is None else jnp.maximum(peak, part)
        peak = jnp.broadcast_to(jnp.max(peak, axis=1, keepdims=True), peak.shape)
        if has_state:
            peak = jnp.maximum(peak, states[index][1][unit])
        return peak

    def mix(index, unit, slot, peak):
        total = None
        for at, step in steps:
            weights = jnp.concatenate(
                [
                    jnp.exp2((scores[slot, :, lane : lane + 128] - peak) * scale).astype(BF16)
                    for lane in range(at, at + step, 128)
                ],
                1,
            )
            part = jnp.dot(weights, extended[at : at + step, :], preferred_element_type=F32)
            total = part if total is None else total + part
        if has_state:
            old_sum, old_peak = states[index]
            decay = jnp.exp2((old_peak[unit] - peak) * scale)
            total = jnp.concatenate(
                [
                    total[:, lane : lane + 128] + old_sum[unit, :, lane : lane + 128] * decay
                    for lane in range(0, padded, 128)
                ],
                1,
            )
        if not last:
            new_sum[unit] = total
            new_peak[unit] = peak
            return
        inverse = jnp.broadcast_to(1.0 / total[:, values : values + 1], peak.shape)
        result = jnp.concatenate(
            [(total[:, lane : lane + 128] * inverse).astype(BF16) for lane in range(0, padded, 128)], 1
        )[:, :values]
        wide = group * values
        mixed[index * rows : (index + 1) * rows, unit * wide : (unit + 1) * wide] = jnp.concatenate(
            [result[i * rows : (i + 1) * rows, :] for i in range(group)], 1
        )

    peak = score(*units[0], 0)
    for at, unit in enumerate(units):
        following = score(*units[at + 1], (at + 1) % 2) if at + 1 < len(units) else None
        mix(*unit, at % 2, peak)
        peak = following
    if last:
        out[...] = product(mixed[...], w_out[...]).astype(BF16)


def attend(queries, pairs, block, keys, values, states=None, w_out=None, place=None, carried=None, weight=1.0, lead=0, drop=0):
    rows = queries[0].shape[0]
    heads = queries[0].shape[1] // keys
    group = 2
    while group * rows < STACKED and heads % (2 * group) == 0:
        group *= 2
    room = sum(pair.shape[0] for pair in pairs) * keys // (keys + values) - (block - lead if lead else 0)
    seen = room - drop
    padded = (values // 128 + 1) * 128
    last = w_out is not None
    shape = (len(queries), [block] * len(pairs), lead, drop, states is not None, last, carried is not None, heads, group, keys, values)
    arguments = list(queries) + list(pairs) + [part for state in states or () for part in state]
    scratch = [
        pltpu.VMEM((room, keys), BF16),
        pltpu.VMEM((room, padded), BF16),
        pltpu.VMEM((2, group * rows, seen), F32),
    ]
    in_specs = [whole()] * len(arguments)
    aliases = {}
    if last:
        index, count = place
        arguments.append(w_out)
        in_specs.append(whole())
        if carried is not None:
            aliases = {len(arguments): 0}
            arguments.append(carried)
            in_specs.append(whole(pl.ANY))
        out_shape = jax.ShapeDtypeStruct((rows * len(queries) * count, w_out.shape[1]), BF16)
        out_specs = pl.BlockSpec((rows * len(queries), w_out.shape[1]), lambda i: (index, 0))
        scratch.append(pltpu.VMEM((rows * len(queries), heads * values), BF16))
    else:
        out_shape = [
            jax.ShapeDtypeStruct((heads // group, group * rows, padded), F32),
            jax.ShapeDtypeStruct((heads // group, group * rows, 128), F32),
        ]
        out_specs = [whole()] * 2
    flops = int(weight * 2 * len(queries) * rows * heads * seen * (keys + values))
    if last:
        flops += 2 * len(queries) * rows * heads * values * w_out.shape[1]
    return pl.pallas_call(
        functools.partial(attend_kernel, shape),
        grid=(1,),
        in_specs=in_specs,
        out_specs=out_specs,
        out_shape=out_shape,
        scratch_shapes=scratch,
        input_output_aliases=aliases,
        compiler_params=pltpu.CompilerParams(vmem_limit_bytes=28 << 20),
        cost_estimate=pl.CostEstimate(
            flops=flops,
            bytes_accessed=2 * seen * (keys + values),
            transcendentals=0,
        ),
        name="attend",
    )(*arguments)


def other_core(value):
    count = lax.axis_size("seq")
    return lax.ppermute(value, "seq", [(s, s ^ 1) for s in range(count)])


def after(value, *others):
    return lax.optimization_barrier((value, *others))[0]


def crossed(value, lane_bit, place_bits):
    lanes, count = lax.axis_size("ws"), lax.axis_size("seq")
    bits = place_bits if isinstance(place_bits, tuple) else (place_bits, place_bits)
    pairs = [
        (w * count + s, (w ^ lane_bit) * count + (s ^ bits[s % 2]))
        for w in range(lanes)
        for s in range(count)
    ]
    return lax.ppermute(value, ("ws", "seq"), pairs)


def spread(block, twin):
    places = list(range(2, lax.axis_size("seq"), 2))
    whole_chip = jnp.concatenate([block, twin], 0)
    single = crossed(block, 0, places[-1])
    return [single] + [
        crossed(whole_chip, 0, (places[i], places[i + 1])) for i in range(0, len(places) - 1, 2)
    ]


def body(tokens, w_same, w_partner, w_query, w_key, w_value, w_out):
    count = lax.axis_size("seq")
    local = tokens[0]
    half = local.shape[0] // 2
    keys, values = w_key.shape[1], w_value.shape[1]
    width = local.shape[1]
    sizes = [width * part // sum(COLUMNS) for part in COLUMNS]
    spans = [(sum(sizes[:i]), size) for i, size in enumerate(sizes)]
    arrived = [crossed(piece, 1, count - 1) for piece in [local[half:, at : at + size] for at, size in spans]]
    same, partner, w_pair = own_products(local, w_same, w_partner, w_key, w_value.T, half)
    for (at, _), piece in zip(spans[:-1], arrived[:-1]):
        same, partner = add_products(at, piece, same, partner, w_same, w_partner)
    hidden, own, other = hidden_and_pairs(
        spans[-1][0], arrived[-1], same, partner, w_same, w_partner, w_pair, keys, values
    )
    places = range(2, count, 2)
    near = [own] + [crossed(own, 0, k) for k in places]
    lifted = crossed(other, 1, 0)
    query, sent = query_rows(hidden, w_query, [half, half])
    near, lifted, query = lax.optimization_barrier((near, lifted, query))
    high = other_core(lifted)
    early = near + [other_core(part) for part in near] + [lifted, high]
    brought = crossed(sent, 1, count - 1)
    spare = len(early) * half % 256 if len(early) * half % 256 <= half else 0
    mine = attend([query], early, half, keys, values, weight=0.7, drop=spare)
    brought = after(brought, mine)
    far = spread(lifted, high)
    theirs = attend([brought], early, half, keys, values, weight=1.0, drop=spare)
    far = after(far, theirs)
    late = far + [other_core(part) for part in far]
    if spare:
        late = [high] + late
    result = attend([query, brought], late, half, keys, values, [mine, theirs], w_out, (0, 1), lead=spare)
    return result[None]


def solution(mesh):
    placed = (P("ws", "seq", None), P(), P(), P(), P(), P(), P())
    return jax.shard_map(
        body, mesh=mesh, in_specs=placed, out_specs=P("ws", "seq", None), check_vma=False
    )
```

```python
import functools
import math

import jax
import jax.numpy as jnp
from jax import lax
from jax.experimental import pallas as pl
from jax.experimental.pallas import tpu as pltpu
from jax.sharding import PartitionSpec as P

F32 = jnp.float32
BF16 = jnp.bfloat16
CONTRACT_LAST = (((1,), (1,)), ((), ()))
STACKED = 384
COLUMNS = (5, 1)


def whole(memory_space=pltpu.VMEM):
    return pl.BlockSpec(memory_space=memory_space)


def reversed_rows(block):
    rows = block.shape[0]
    row = lax.broadcasted_iota(jnp.int32, (rows, rows), 0)
    column = lax.broadcasted_iota(jnp.int32, (rows, rows), 1)
    swap = (row + column == rows - 1).astype(F32).astype(BF16)
    return jnp.dot(swap, block, preferred_element_type=F32).astype(BF16)


def product(left, right):
    return jnp.dot(left, right, preferred_element_type=F32)


def own_kernel(tokens, w_same, w_partner, w_key, w_value, same, partner, w_pair):
    rows, keys = same.shape[0], w_key.shape[1]
    w_pair[:, :keys] = w_key[...]
    w_pair[:, keys : keys + w_value.shape[0]] = w_value[...].T
    w_pair[:, keys + w_value.shape[0] :] = jnp.zeros(
        (w_pair.shape[0], w_pair.shape[1] - keys - w_value.shape[0]), BF16
    )
    block = tokens[:rows, :]
    same[...] = product(block, w_same[...])
    partner[...] = product(reversed_rows(block), w_partner[...])


def own_products(tokens, w_same, w_partner, w_key, w_value, rows):
    width, features = w_same.shape
    both = -(-(w_key.shape[1] + w_value.shape[0]) // 128) * 128
    return pl.pallas_call(
        own_kernel,
        in_specs=[whole()] * 5,
        out_specs=[whole()] * 3,
        out_shape=[jax.ShapeDtypeStruct((rows, features), F32)] * 2
        + [jax.ShapeDtypeStruct((width, both), BF16)],
        compiler_params=pltpu.CompilerParams(vmem_limit_bytes=20 << 20),
        cost_estimate=pl.CostEstimate(
            flops=4 * rows * width * features, bytes_accessed=4 * width * features, transcendentals=0
        ),
        name="own_products",
    )(tokens, w_same, w_partner, w_key, w_value)


def pack(pair, value, rows, lanes):
    width = value.shape[1]
    at = rows
    for lane in range(0, width - width % lanes, lanes):
        pair[at : at + rows, :] = value[:, lane : lane + lanes]
        at += rows
    rest = width % lanes
    if rest:
        share = rows * rest // lanes
        pair[at : at + share, :] = jnp.concatenate(
            [value[i * share : (i + 1) * share, width - rest :] for i in range(lanes // rest)], 1
        )


def unpack(pair, at, rows, lanes, width):
    key = pair[at : at + rows, :]
    at += rows
    parts = []
    for _ in range(width // lanes):
        parts.append(pair[at : at + rows, :])
        at += rows
    rest = width % lanes
    if rest:
        share = rows * rest // lanes
        tail = pair[at : at + share, :]
        parts.append(
            jnp.concatenate([tail[:, i * rest : (i + 1) * rest] for i in range(lanes // rest)], 0)
        )
    return key, jnp.concatenate(parts, 1)


def add_kernel(at, arrived, same, partner, w_same, w_partner, upper, lower):
    block = arrived[...]
    depth = pl.ds(at, block.shape[1])
    upper[...] = same[...] + product(reversed_rows(block), w_partner[depth, :])
    lower[...] = partner[...] + product(block, w_same[depth, :])


def add_products(at, arrived, same, partner, w_same, w_partner):
    rows, width = arrived.shape
    features = w_same.shape[1]
    return pl.pallas_call(
        functools.partial(add_kernel, at),
        in_specs=[whole()] * 5,
        out_specs=[whole()] * 2,
        out_shape=[jax.ShapeDtypeStruct((rows, features), F32)] * 2,
        compiler_params=pltpu.CompilerParams(vmem_limit_bytes=20 << 20),
        cost_estimate=pl.CostEstimate(
            flops=4 * rows * width * features, bytes_accessed=4 * width * features, transcendentals=0
        ),
        name="add_products",
    )(arrived, same, partner, w_same, w_partner)


def hidden_kernel(keys, values, at, arrived, same, partner, w_same, w_partner, w_pair, hidden, own, other):
    rows = arrived.shape[0]
    block = arrived[...]
    depth = pl.ds(at, block.shape[1])
    upper = (same[...] + product(reversed_rows(block), w_partner[depth, :])).astype(BF16)
    lower = (partner[...] + product(block, w_same[depth, :])).astype(BF16)
    hidden[:rows, :] = upper
    hidden[rows:, :] = lower
    both = jnp.concatenate([upper, lower], 0)
    result = product(both, w_pair[...]).astype(BF16)
    for pair, first in ((own, 0), (other, rows)):
        pair[:rows, :] = result[first : first + rows, :keys]
        pack(pair, result[first : first + rows, keys : keys + values], rows, keys)


def hidden_and_pairs(at, arrived, same, partner, w_same, w_partner, w_pair, keys, values):
    rows, width = arrived.shape
    features = w_same.shape[1]
    pair = jax.ShapeDtypeStruct((rows * (keys + values) // keys, keys), BF16)
    return pl.pallas_call(
        functools.partial(hidden_kernel, keys, values, at),
        in_specs=[whole()] * 6,
        out_specs=[whole()] * 3,
        out_shape=[jax.ShapeDtypeStruct((2 * rows, features), BF16), pair, pair],
        compiler_params=pltpu.CompilerParams(vmem_limit_bytes=20 << 20),
        cost_estimate=pl.CostEstimate(
            flops=4 * rows * (width * features + features * (keys + values)),
            bytes_accessed=4 * width * features,
            transcendentals=0,
        ),
        name="hidden_and_pairs",
    )(arrived, same, partner, w_same, w_partner, w_pair)


def query_kernel(hidden, w_query, *queries):
    result = product(hidden[...], w_query[...]).astype(BF16)
    at = 0
    for query in queries:
        query[...] = result[at : at + query.shape[0], :]
        at += query.shape[0]


def query_rows(hidden, w_query, sizes):
    width, queries = w_query.shape
    return pl.pallas_call(
        query_kernel,
        in_specs=[whole()] * 2,
        out_specs=[whole()] * len(sizes),
        out_shape=[jax.ShapeDtypeStruct((size, queries), BF16) for size in sizes],
        compiler_params=pltpu.CompilerParams(vmem_limit_bytes=16 << 20),
        cost_estimate=pl.CostEstimate(
            flops=2 * hidden.shape[0] * width * queries,
            bytes_accessed=2 * width * queries,
            transcendentals=0,
        ),
        name="query_rows",
    )(hidden, w_query)


def attend_kernel(shape, *refs):
    n_query, blocks, lead, drop, has_state, last, carried, heads, group, keys, values = shape
    refs = list(refs)
    queries = [refs.pop(0) for _ in range(n_query)]
    pairs = [refs.pop(0) for _ in blocks]
    states = [(refs.pop(0), refs.pop(0)) for _ in range(n_query if has_state else 0)]
    if last:
        w_out = refs.pop(0)
        if carried:
            refs.pop(0)
        out = refs.pop(0)
    else:
        new_sum, new_peak = refs.pop(0), refs.pop(0)
    held, extended, scores = refs.pop(0), refs.pop(0), refs.pop(0)
    if last:
        mixed = refs.pop(0)
    rows = queries[0].shape[0]
    units = [(index, unit) for index in range(n_query) for unit in range(heads // group)]
    padded = extended.shape[1]
    scale = keys**-0.5 * math.log2(math.e)
    seen = 0
    for pair, block in zip(pairs, blocks):
        packed = block * (keys + values) // keys
        for at in range(0, pair.shape[0], packed):
            key, value = unpack(pair, at, block, keys, values)
            taken = lead if lead and not seen else block
            held[seen : seen + taken, :] = key[block - taken :, :]
            extended[seen : seen + taken, :values] = value[block - taken :, :]
            seen += taken
    extended[:, values:] = jnp.ones((seen, padded - values), BF16)
    seen -= drop
    steps = [(at, min(512, seen - at)) for at in range(0, seen, 512)]

    def score(index, unit, slot):
        wide = group * keys
        columns = queries[index][:, unit * wide : (unit + 1) * wide]
        stacked = jnp.concatenate([columns[:, i * keys : (i + 1) * keys] for i in range(group)], 0)
        peak = None
        for at, step in steps:
            block = lax.dot_general(
                stacked, held[at : at + step, :], CONTRACT_LAST, preferred_element_type=F32
            )
            scores[slot, :, at : at + step] = block
            for lane in range(0, step, 128):
                part = block[:, lane : lane + 128]
                peak = part if peak is None else jnp.maximum(peak, part)
        peak = jnp.broadcast_to(jnp.max(peak, axis=1, keepdims=True), peak.shape)
        if has_state:
            peak = jnp.maximum(peak, states[index][1][unit])
        return peak

    def mix(index, unit, slot, peak):
        total = None
        for at, step in steps:
            weights = jnp.concatenate(
                [
                    jnp.exp2((scores[slot, :, lane : lane + 128] - peak) * scale).astype(BF16)
                    for lane in range(at, at + step, 128)
                ],
                1,
            )
            part = jnp.dot(weights, extended[at : at + step, :], preferred_element_type=F32)
            total = part if total is None else total + part
        if has_state:
            old_sum, old_peak = states[index]
            decay = jnp.exp2((old_peak[unit] - peak) * scale)
            total = jnp.concatenate(
                [
                    total[:, lane : lane + 128] + old_sum[unit, :, lane : lane + 128] * decay
                    for lane in range(0, padded, 128)
                ],
                1,
            )
        if not last:
            new_sum[unit] = total
            new_peak[unit] = peak
            return
        inverse = jnp.broadcast_to(1.0 / total[:, values : values + 1], peak.shape)
        result = jnp.concatenate(
            [(total[:, lane : lane + 128] * inverse).astype(BF16) for lane in range(0, padded, 128)], 1
        )[:, :values]
        wide = group * values
        mixed[index * rows : (index + 1) * rows, unit * wide : (unit + 1) * wide] = jnp.concatenate(
            [result[i * rows : (i + 1) * rows, :] for i in range(group)], 1
        )

    peak = score(*units[0], 0)
    for at, unit in enumerate(units):
        following = score(*units[at + 1], (at + 1) % 2) if at + 1 < len(units) else None
        mix(*unit, at % 2, peak)
        peak = following
    if last:
        out[...] = product(mixed[...], w_out[...]).astype(BF16)


def attend(queries, pairs, block, keys, values, states=None, w_out=None, place=None, carried=None, weight=1.0, lead=0, drop=0):
    rows = queries[0].shape[0]
    heads = queries[0].shape[1] // keys
    group = 2
    while group * rows < STACKED and heads % (2 * group) == 0:
        group *= 2
    room = sum(pair.shape[0] for pair in pairs) * keys // (keys + values) - (block - lead if lead else 0)
    seen = room - drop
    padded = (values // 128 + 1) * 128
    last = w_out is not None
    shape = (len(queries), [block] * len(pairs), lead, drop, states is not None, last, carried is not None, heads, group, keys, values)
    arguments = list(queries) + list(pairs) + [part for state in states or () for part in state]
    scratch = [
        pltpu.VMEM((room, keys), BF16),
        pltpu.VMEM((room, padded), BF16),
        pltpu.VMEM((2, group * rows, seen), F32),
    ]
    in_specs = [whole()] * len(arguments)
    aliases = {}
    if last:
        index, count = place
        arguments.append(w_out)
        in_specs.append(whole())
        if carried is not None:
            aliases = {len(arguments): 0}
            arguments.append(carried)
            in_specs.append(whole(pl.ANY))
        out_shape = jax.ShapeDtypeStruct((rows * len(queries) * count, w_out.shape[1]), BF16)
        out_specs = pl.BlockSpec((rows * len(queries), w_out.shape[1]), lambda i: (index, 0))
        scratch.append(pltpu.VMEM((rows * len(queries), heads * values), BF16))
    else:
        out_shape = [
            jax.ShapeDtypeStruct((heads // group, group * rows, padded), F32),
            jax.ShapeDtypeStruct((heads // group, group * rows, 128), F32),
        ]
        out_specs = [whole()] * 2
    flops = int(weight * 2 * len(queries) * rows * heads * seen * (keys + values))
    if last:
        flops += 2 * len(queries) * rows * heads * values * w_out.shape[1]
    return pl.pallas_call(
        functools.partial(attend_kernel, shape),
        grid=(1,),
        in_specs=in_specs,
        out_specs=out_specs,
        out_shape=out_shape,
        scratch_shapes=scratch,
        input_output_aliases=aliases,
        compiler_params=pltpu.CompilerParams(vmem_limit_bytes=28 << 20),
        cost_estimate=pl.CostEstimate(
            flops=flops,
            bytes_accessed=2 * seen * (keys + values),
            transcendentals=0,
        ),
        name="attend",
    )(*arguments)


def other_core(value):
    count = lax.axis_size("seq")
    return lax.ppermute(value, "seq", [(s, s ^ 1) for s in range(count)])


def after(value, *others):
    return lax.optimization_barrier((value, *others))[0]


def crossed(value, lane_bit, place_bits):
    lanes, count = lax.axis_size("ws"), lax.axis_size("seq")
    bits = place_bits if isinstance(place_bits, tuple) else (place_bits, place_bits)
    pairs = [
        (w * count + s, (w ^ lane_bit) * count + (s ^ bits[s % 2]))
        for w in range(lanes)
        for s in range(count)
    ]
    return lax.ppermute(value, ("ws", "seq"), pairs)


def spread(block, twin, places):
    whole_chip = jnp.concatenate([block, twin], 0)
    return [crossed(whole_chip, 0, (places[i], places[i + 1])) for i in range(0, len(places), 2)]


def body(tokens, w_same, w_partner, w_query, w_key, w_value, w_out):
    count = lax.axis_size("seq")
    local = tokens[0]
    half = local.shape[0] // 2
    keys, values = w_key.shape[1], w_value.shape[1]
    width = local.shape[1]
    sizes = [width * part // sum(COLUMNS) for part in COLUMNS]
    spans = [(sum(sizes[:i]), size) for i, size in enumerate(sizes)]
    arrived = [crossed(piece, 1, count - 1) for piece in [local[half:, at : at + size] for at, size in spans]]
    same, partner, w_pair = own_products(local, w_same, w_partner, w_key, w_value.T, half)
    for (at, _), piece in zip(spans[:-1], arrived[:-1]):
        same, partner = add_products(at, piece, same, partner, w_same, w_partner)
    hidden, own, other = hidden_and_pairs(
        spans[-1][0], arrived[-1], same, partner, w_same, w_partner, w_pair, keys, values
    )
    places = range(2, count, 2)
    near = [own] + [crossed(own, 0, k) for k in places]
    lifted = crossed(other, 1, 0)
    across = crossed(other, 1, count - 1)
    query, sent = query_rows(hidden, w_query, [half, half])
    near, lifted, across, query = lax.optimization_barrier((near, lifted, across, query))
    high = other_core(lifted)
    early = near + [across]
    early = early + [other_core(part) for part in early] + [lifted, high]
    brought = crossed(sent, 1, count - 1)
    spare = len(early) * half % 256 if len(early) * half % 256 <= half else 0
    mine = attend([query], early, half, keys, values, weight=0.5, drop=spare)
    brought = after(brought, mine)
    far = spread(lifted, high, places[:-1])
    theirs = attend([brought], early, half, keys, values, weight=1.0, drop=spare)
    far = after(far, theirs)
    late = far + [other_core(part) for part in far]
    if spare:
        late = [high] + late
    result = attend([query, brought], late, half, keys, values, [mine, theirs], w_out, (0, 1), lead=spare)
    return result[None]


def solution(mesh):
    placed = (P("ws", "seq", None), P(), P(), P(), P(), P(), P())
    return jax.shard_map(
        body, mesh=mesh, in_specs=placed, out_specs=P("ws", "seq", None), check_vma=False
    )
```

```python
import functools
import math

import jax
import jax.numpy as jnp
from jax import lax
from jax.experimental import pallas as pl
from jax.experimental.pallas import tpu as pltpu
from jax.sharding import PartitionSpec as P

F32 = jnp.float32
BF16 = jnp.bfloat16
CONTRACT_LAST = (((1,), (1,)), ((), ()))
STACKED = 384
COLUMNS = (5, 1)


def whole(memory_space=pltpu.VMEM):
    return pl.BlockSpec(memory_space=memory_space)


def reversed_rows(block):
    rows = block.shape[0]
    row = lax.broadcasted_iota(jnp.int32, (rows, rows), 0)
    column = lax.broadcasted_iota(jnp.int32, (rows, rows), 1)
    swap = (row + column == rows - 1).astype(F32).astype(BF16)
    return jnp.dot(swap, block, preferred_element_type=F32).astype(BF16)


def product(left, right):
    return jnp.dot(left, right, preferred_element_type=F32)


def own_kernel(tokens, w_same, w_partner, w_key, w_value, same, partner, w_pair):
    rows, keys = same.shape[0], w_key.shape[1]
    w_pair[:, :keys] = w_key[...]
    w_pair[:, keys : keys + w_value.shape[0]] = w_value[...].T
    w_pair[:, keys + w_value.shape[0] :] = jnp.zeros(
        (w_pair.shape[0], w_pair.shape[1] - keys - w_value.shape[0]), BF16
    )
    block = tokens[:rows, :]
    same[...] = product(block, w_same[...])
    partner[...] = product(reversed_rows(block), w_partner[...])


def own_products(tokens, w_same, w_partner, w_key, w_value, rows):
    width, features = w_same.shape
    both = -(-(w_key.shape[1] + w_value.shape[0]) // 128) * 128
    return pl.pallas_call(
        own_kernel,
        in_specs=[whole()] * 5,
        out_specs=[whole()] * 3,
        out_shape=[jax.ShapeDtypeStruct((rows, features), F32)] * 2
        + [jax.ShapeDtypeStruct((width, both), BF16)],
        compiler_params=pltpu.CompilerParams(vmem_limit_bytes=20 << 20),
        cost_estimate=pl.CostEstimate(
            flops=4 * rows * width * features, bytes_accessed=4 * width * features, transcendentals=0
        ),
        name="own_products",
    )(tokens, w_same, w_partner, w_key, w_value)


def pack(pair, value, rows, lanes):
    width = value.shape[1]
    at = rows
    for lane in range(0, width - width % lanes, lanes):
        pair[at : at + rows, :] = value[:, lane : lane + lanes]
        at += rows
    rest = width % lanes
    if rest:
        share = rows * rest // lanes
        pair[at : at + share, :] = jnp.concatenate(
            [value[i * share : (i + 1) * share, width - rest :] for i in range(lanes // rest)], 1
        )


def unpack(pair, at, rows, lanes, width):
    key = pair[at : at + rows, :]
    at += rows
    parts = []
    for _ in range(width // lanes):
        parts.append(pair[at : at + rows, :])
        at += rows
    rest = width % lanes
    if rest:
        share = rows * rest // lanes
        tail = pair[at : at + share, :]
        parts.append(
            jnp.concatenate([tail[:, i * rest : (i + 1) * rest] for i in range(lanes // rest)], 0)
        )
    return key, jnp.concatenate(parts, 1)


def add_kernel(at, arrived, same, partner, w_same, w_partner, upper, lower):
    block = arrived[...]
    depth = pl.ds(at, block.shape[1])
    upper[...] = same[...] + product(reversed_rows(block), w_partner[depth, :])
    lower[...] = partner[...] + product(block, w_same[depth, :])


def add_products(at, arrived, same, partner, w_same, w_partner):
    rows, width = arrived.shape
    features = w_same.shape[1]
    return pl.pallas_call(
        functools.partial(add_kernel, at),
        in_specs=[whole()] * 5,
        out_specs=[whole()] * 2,
        out_shape=[jax.ShapeDtypeStruct((rows, features), F32)] * 2,
        compiler_params=pltpu.CompilerParams(vmem_limit_bytes=20 << 20),
        cost_estimate=pl.CostEstimate(
            flops=4 * rows * width * features, bytes_accessed=4 * width * features, transcendentals=0
        ),
        name="add_products",
    )(arrived, same, partner, w_same, w_partner)


def hidden_kernel(keys, values, at, arrived, same, partner, w_same, w_partner, w_pair, hidden, own, other):
    rows = arrived.shape[0]
    block = arrived[...]
    depth = pl.ds(at, block.shape[1])
    upper = (same[...] + product(reversed_rows(block), w_partner[depth, :])).astype(BF16)
    lower = (partner[...] + product(block, w_same[depth, :])).astype(BF16)
    hidden[:rows, :] = upper
    hidden[rows:, :] = lower
    both = jnp.concatenate([upper, lower], 0)
    result = product(both, w_pair[...]).astype(BF16)
    for pair, first in ((own, 0), (other, rows)):
        pair[:rows, :] = result[first : first + rows, :keys]
        pack(pair, result[first : first + rows, keys : keys + values], rows, keys)


def hidden_and_pairs(at, arrived, same, partner, w_same, w_partner, w_pair, keys, values):
    rows, width = arrived.shape
    features = w_same.shape[1]
    pair = jax.ShapeDtypeStruct((rows * (keys + values) // keys, keys), BF16)
    return pl.pallas_call(
        functools.partial(hidden_kernel, keys, values, at),
        in_specs=[whole()] * 6,
        out_specs=[whole()] * 3,
        out_shape=[jax.ShapeDtypeStruct((2 * rows, features), BF16), pair, pair],
        compiler_params=pltpu.CompilerParams(vmem_limit_bytes=20 << 20),
        cost_estimate=pl.CostEstimate(
            flops=4 * rows * (width * features + features * (keys + values)),
            bytes_accessed=4 * width * features,
            transcendentals=0,
        ),
        name="hidden_and_pairs",
    )(arrived, same, partner, w_same, w_partner, w_pair)


def query_kernel(hidden, w_query, *queries):
    result = product(hidden[...], w_query[...]).astype(BF16)
    at = 0
    for query in queries:
        query[...] = result[at : at + query.shape[0], :]
        at += query.shape[0]


def query_rows(hidden, w_query, sizes):
    width, queries = w_query.shape
    return pl.pallas_call(
        query_kernel,
        in_specs=[whole()] * 2,
        out_specs=[whole()] * len(sizes),
        out_shape=[jax.ShapeDtypeStruct((size, queries), BF16) for size in sizes],
        compiler_params=pltpu.CompilerParams(vmem_limit_bytes=16 << 20),
        cost_estimate=pl.CostEstimate(
            flops=2 * hidden.shape[0] * width * queries,
            bytes_accessed=2 * width * queries,
            transcendentals=0,
        ),
        name="query_rows",
    )(hidden, w_query)


def attend_kernel(shape, *refs):
    n_query, blocks, lead, drop, has_state, last, carried, heads, group, keys, values = shape
    refs = list(refs)
    queries = [refs.pop(0) for _ in range(n_query)]
    pairs = [refs.pop(0) for _ in blocks]
    states = [(refs.pop(0), refs.pop(0)) for _ in range(n_query if has_state else 0)]
    if last:
        w_out = refs.pop(0)
        if carried:
            refs.pop(0)
        out = refs.pop(0)
    else:
        new_sum, new_peak = refs.pop(0), refs.pop(0)
    held, extended, scores = refs.pop(0), refs.pop(0), refs.pop(0)
    if last:
        mixed = refs.pop(0)
    rows = queries[0].shape[0]
    units = [(index, unit) for index in range(n_query) for unit in range(heads // group)]
    padded = extended.shape[1]
    scale = keys**-0.5 * math.log2(math.e)
    seen = 0
    for pair, block in zip(pairs, blocks):
        packed = block * (keys + values) // keys
        for at in range(0, pair.shape[0], packed):
            key, value = unpack(pair, at, block, keys, values)
            taken = lead if lead and not seen else block
            held[seen : seen + taken, :] = key[block - taken :, :]
            extended[seen : seen + taken, :values] = value[block - taken :, :]
            seen += taken
    extended[:, values:] = jnp.ones((seen, padded - values), BF16)
    seen -= drop
    steps = [(at, min(512, seen - at)) for at in range(0, seen, 512)]

    def score(index, unit, slot):
        wide = group * keys
        columns = queries[index][:, unit * wide : (unit + 1) * wide]
        stacked = jnp.concatenate([columns[:, i * keys : (i + 1) * keys] for i in range(group)], 0)
        peak = None
        for at, step in steps:
            block = lax.dot_general(
                stacked, held[at : at + step, :], CONTRACT_LAST, preferred_element_type=F32
            )
            scores[slot, :, at : at + step] = block
            for lane in range(0, step, 128):
                part = block[:, lane : lane + 128]
                peak = part if peak is None else jnp.maximum(peak, part)
        peak = jnp.broadcast_to(jnp.max(peak, axis=1, keepdims=True), peak.shape)
        if has_state:
            peak = jnp.maximum(peak, states[index][1][unit])
        return peak

    def mix(index, unit, slot, peak):
        total = None
        for at, step in steps:
            weights = jnp.concatenate(
                [
                    jnp.exp2((scores[slot, :, lane : lane + 128] - peak) * scale).astype(BF16)
                    for lane in range(at, at + step, 128)
                ],
                1,
            )
            part = jnp.dot(weights, extended[at : at + step, :], preferred_element_type=F32)
            total = part if total is None else total + part
        if has_state:
            old_sum, old_peak = states[index]
            decay = jnp.exp2((old_peak[unit] - peak) * scale)
            total = jnp.concatenate(
                [
                    total[:, lane : lane + 128] + old_sum[unit, :, lane : lane + 128] * decay
                    for lane in range(0, padded, 128)
                ],
                1,
            )
        if not last:
            new_sum[unit] = total
            new_peak[unit] = peak
            return
        inverse = jnp.broadcast_to(1.0 / total[:, values : values + 1], peak.shape)
        result = jnp.concatenate(
            [(total[:, lane : lane + 128] * inverse).astype(BF16) for lane in range(0, padded, 128)], 1
        )[:, :values]
        wide = group * values
        mixed[index * rows : (index + 1) * rows, unit * wide : (unit + 1) * wide] = jnp.concatenate(
            [result[i * rows : (i + 1) * rows, :] for i in range(group)], 1
        )

    peak = score(*units[0], 0)
    for at, unit in enumerate(units):
        following = score(*units[at + 1], (at + 1) % 2) if at + 1 < len(units) else None
        mix(*unit, at % 2, peak)
        peak = following
    if last:
        out[...] = product(mixed[...], w_out[...]).astype(BF16)


def attend(queries, pairs, block, keys, values, states=None, w_out=None, place=None, carried=None, weight=1.0, lead=0, drop=0):
    rows = queries[0].shape[0]
    heads = queries[0].shape[1] // keys
    group = 2
    while group * rows < STACKED and heads % (2 * group) == 0:
        group *= 2
    room = sum(pair.shape[0] for pair in pairs) * keys // (keys + values) - (block - lead if lead else 0)
    seen = room - drop
    padded = (values // 128 + 1) * 128
    last = w_out is not None
    shape = (len(queries), [block] * len(pairs), lead, drop, states is not None, last, carried is not None, heads, group, keys, values)
    arguments = list(queries) + list(pairs) + [part for state in states or () for part in state]
    scratch = [
        pltpu.VMEM((room, keys), BF16),
        pltpu.VMEM((room, padded), BF16),
        pltpu.VMEM((2, group * rows, seen), F32),
    ]
    in_specs = [whole()] * len(arguments)
    aliases = {}
    if last:
        index, count = place
        arguments.append(w_out)
        in_specs.append(whole())
        if carried is not None:
            aliases = {len(arguments): 0}
            arguments.append(carried)
            in_specs.append(whole(pl.ANY))
        out_shape = jax.ShapeDtypeStruct((rows * len(queries) * count, w_out.shape[1]), BF16)
        out_specs = pl.BlockSpec((rows * len(queries), w_out.shape[1]), lambda i: (index, 0))
        scratch.append(pltpu.VMEM((rows * len(queries), heads * values), BF16))
    else:
        out_shape = [
            jax.ShapeDtypeStruct((heads // group, group * rows, padded), F32),
            jax.ShapeDtypeStruct((heads // group, group * rows, 128), F32),
        ]
        out_specs = [whole()] * 2
    flops = int(weight * 2 * len(queries) * rows * heads * seen * (keys + values))
    if last:
        flops += 2 * len(queries) * rows * heads * values * w_out.shape[1]
    return pl.pallas_call(
        functools.partial(attend_kernel, shape),
        grid=(1,),
        in_specs=in_specs,
        out_specs=out_specs,
        out_shape=out_shape,
        scratch_shapes=scratch,
        input_output_aliases=aliases,
        compiler_params=pltpu.CompilerParams(vmem_limit_bytes=28 << 20),
        cost_estimate=pl.CostEstimate(
            flops=flops,
            bytes_accessed=2 * seen * (keys + values),
            transcendentals=0,
        ),
        name="attend",
    )(*arguments)


def other_core(value):
    count = lax.axis_size("seq")
    return lax.ppermute(value, "seq", [(s, s ^ 1) for s in range(count)])


def after(value, *others):
    return lax.optimization_barrier((value, *others))[0]


def crossed(value, lane_bit, place_bits):
    lanes, count = lax.axis_size("ws"), lax.axis_size("seq")
    bits = place_bits if isinstance(place_bits, tuple) else (place_bits, place_bits)
    pairs = [
        (w * count + s, (w ^ lane_bit) * count + (s ^ bits[s % 2]))
        for w in range(lanes)
        for s in range(count)
    ]
    return lax.ppermute(value, ("ws", "seq"), pairs)


def spread(block, twin, places):
    whole_chip = jnp.concatenate([block, twin], 0)
    return [crossed(whole_chip, 0, (places[i], places[i + 1])) for i in range(0, len(places), 2)]


def body(tokens, w_same, w_partner, w_query, w_key, w_value, w_out):
    count = lax.axis_size("seq")
    local = tokens[0]
    half = local.shape[0] // 2
    keys, values = w_key.shape[1], w_value.shape[1]
    width = local.shape[1]
    sizes = [width * part // sum(COLUMNS) for part in COLUMNS]
    spans = [(sum(sizes[:i]), size) for i, size in enumerate(sizes)]
    arrived = [crossed(piece, 1, count - 1) for piece in [local[half:, at : at + size] for at, size in spans]]
    same, partner, w_pair = own_products(local, w_same, w_partner, w_key, w_value.T, half)
    for (at, _), piece in zip(spans[:-1], arrived[:-1]):
        same, partner = add_products(at, piece, same, partner, w_same, w_partner)
    hidden, own, other = hidden_and_pairs(
        spans[-1][0], arrived[-1], same, partner, w_same, w_partner, w_pair, keys, values
    )
    places = range(2, count, 2)
    near = [own] + [crossed(own, 0, k) for k in places]
    across = crossed(other, 1, count - 1)
    lifted = crossed(other, 1, 0)
    query, sent = query_rows(hidden, w_query, [half, half])
    near, lifted, query = lax.optimization_barrier((near, lifted, query))
    across = after(across, query)
    high = other_core(lifted)
    early = near + [across]
    early = early + [other_core(part) for part in early] + [lifted, high]
    brought = crossed(sent, 1, count - 1)
    spare = len(early) * half % 256 if len(early) * half % 256 <= half else 0
    mine = attend([query], early, half, keys, values, weight=0.5, drop=spare)
    brought = after(brought, mine)
    far = spread(lifted, high, places[:-1])
    theirs = attend([brought], early, half, keys, values, weight=1.0, drop=spare)
    far = after(far, theirs)
    late = far + [other_core(part) for part in far]
    if spare:
        late = [high] + late
    result = attend([query, brought], late, half, keys, values, [mine, theirs], w_out, (0, 1), lead=spare)
    return result[None]


def solution(mesh):
    placed = (P("ws", "seq", None), P(), P(), P(), P(), P(), P())
    return jax.shard_map(
        body, mesh=mesh, in_specs=placed, out_specs=P("ws", "seq", None), check_vma=False
    )
```
